512 devices in a mesh: uly: 8 (over x, z_lo), blk: 64 (over y, z_hi, core).
Axes of the slice: x: 4, y: 8, z: 8 (z_hi: 4, z_lo: 2; z = z_hi * 2 + z_lo), core: 2. Of those that a mesh axis runs over, the one named last changes fastest.
Arguments:
- queries: bfloat16 [16384, 3072], P(('uly', 'blk')), may hold values from -8 to 8
- keys: bfloat16 [16384, 3072], P(('uly', 'blk')), may hold values from -8 to 8
- values: bfloat16 [16384, 3072], P(('uly', 'blk')), may hold values from -6 to 6
Outputs:
- attended: bfloat16 [16384, 3072], P(('uly', 'blk'))
The draws below stay inside these ranges and needn't reach their ends.
All inputs are finite; a program needn't handle non-finite values.
Results may differ from the reference program's by a relative error of at most 0.025.
Values may be sent and summed in bfloat16 or wider, within the bound.
No kernel may reach another device: no remote copies, remote signals or barrier semaphores. Data moves between devices by JAX's collectives and lax.ppermute only.
A program may use at most 64 MiB of HBM per device.

```python
import math
import jax
import jax.numpy as jnp
from jax import lax

HEAD_DIM = 128
HEADS = 24
TOKENS = 16384


def draw_queries(key, part):
    key = jax.random.fold_in(key, 11)
    width = HEADS * HEAD_DIM
    base_vals = jnp.clip(jax.random.normal(key, (TOKENS, width), jnp.float32), -8.0, 8.0)
    return base_vals.astype(jnp.bfloat16)


def draw_keys(key, part):
    key = jax.random.fold_in(key, 23)
    width = HEADS * HEAD_DIM
    base_vals = jnp.clip(jax.random.normal(key, (TOKENS, width), jnp.float32), -8.0, 8.0)
    return base_vals.astype(jnp.bfloat16)


def block_levels(rng, dims, cuts, least, top_value):
    factor_of, own = 1.0, jax.random.fold_in(rng, 6)
    for dim, blocks in cuts:
        draws = jnp.exp(jax.random.uniform(jax.random.fold_in(own, dim), (blocks,), jnp.float32, least / len(cuts), top_value / len(cuts)))
        factor_of = factor_of * jnp.repeat(draws, dims[dim] // blocks).reshape([-1 if axis == dim else 1 for axis in range(len(dims))])
    return factor_of


def normal_values(key, shape, spread, bound, cuts=(), held_as=jnp.bfloat16):
    drawn = spread * jax.random.normal(key, shape, jnp.float32)
    if cuts:
        drawn = drawn * block_levels(key, shape, cuts, -0.22, 0.18)
    return jnp.clip(drawn, -bound, bound).astype(held_as)


def setup_inputs(seed: int = 0) -> dict:
    arg_keys = jax.random.split(jax.random.key(seed), 4)
    queries = draw_queries(jax.random.fold_in(arg_keys[3], 71), 0)
    keys = draw_keys(jax.random.fold_in(arg_keys[3], 71), 0)
    values = normal_values(arg_keys[2], (TOKENS, HEADS * HEAD_DIM), 1.0, 6.0, ((0, 512),))
    return {"queries": queries, "keys": keys, "values": values}


def head_attention(stacked):
    q_head, k_head, v_head = stacked
    scale = HEAD_DIM ** -0.5
    block = math.gcd(1024, TOKENS)
    q_blocks = q_head.reshape(TOKENS // block, block, HEAD_DIM)

    def one_block(q_block):
        scores = jnp.dot(q_block, k_head.T, preferred_element_type=jnp.float32) * scale
        row_max = jnp.max(scores, axis=1, keepdims=True)
        expo_vals = jnp.exp(scores - row_max)
        denom = jnp.sum(expo_vals, axis=1, keepdims=True)
        probs = expo_vals.astype(jnp.bfloat16)
        result = jnp.dot(probs, v_head, preferred_element_type=jnp.float32) / denom
        return result.astype(jnp.bfloat16)

    return lax.map(one_block, q_blocks).reshape(TOKENS, HEAD_DIM)


def reference(queries, keys, values):
    def split_heads(array):
        return array.reshape(TOKENS, HEADS, HEAD_DIM).transpose(1, 0, 2)

    per_head = lax.map(head_attention, (split_heads(queries), split_heads(keys), split_heads(values)))
    return per_head.transpose(1, 0, 2).reshape(TOKENS, HEADS * HEAD_DIM)
```

```python
import functools
import math

import jax
import jax.numpy as jnp
from jax import lax
from jax.experimental import pallas as pl
from jax.experimental.pallas import tpu as pltpu
from jax.sharding import Mesh, PartitionSpec as P

HEAD_DIM = 128
STAT_ROWS = 16
EXPONENT = HEAD_DIM**-0.5 * math.log2(math.e)


def attend_kernel(q_ref, kv_ref, out_ref):
    rows = q_ref.shape[0]
    heads = q_ref.shape[1] // HEAD_DIM
    keys_n = kv_ref.shape[0] * kv_ref.shape[2]
    shifts, totals = [], []
    for h in range(heads):
        cols = slice(h * HEAD_DIM, (h + 1) * HEAD_DIM)
        k = kv_ref[:, 0, :, cols].reshape(keys_n, HEAD_DIM)
        v = kv_ref[:, 1, :, cols].reshape(keys_n, HEAD_DIM)
        s = lax.dot_general(
            q_ref[:, cols], k, (((1,), (1,)), ((), ())), preferred_element_type=jnp.float32
        )
        top = jnp.max(s, axis=1, keepdims=True) * EXPONENT
        shift = top.astype(jnp.bfloat16).astype(jnp.float32)
        e = jnp.exp2(s * EXPONENT - shift)
        total = jnp.sum(e, axis=1, keepdims=True)
        o = jnp.dot(e.astype(jnp.bfloat16), v, preferred_element_type=jnp.float32)
        out_ref[0, 0:rows, cols] = o.astype(jnp.bfloat16)
        shifts.append(shift)
        totals.append(total)
    lane = lax.broadcasted_iota(jnp.int32, (rows, HEAD_DIM), 1)
    stats = jnp.zeros((rows, HEAD_DIM), jnp.float32)
    for h in range(heads):
        high = totals[h].astype(jnp.bfloat16).astype(jnp.float32)
        stats = jnp.where(lane == h, shifts[h], stats)
        stats = jnp.where(lane == heads + h, high, stats)
        stats = jnp.where(lane == 2 * heads + h, totals[h] - high, stats)
    out_ref[0, rows : rows + STAT_ROWS, 0:rows] = stats.T[0:STAT_ROWS].astype(jnp.bfloat16)
    out_ref[0, rows : rows + STAT_ROWS, rows:] = jnp.zeros(
        (STAT_ROWS, out_ref.shape[2] - rows), jnp.bfloat16
    )


def attend(q, kv):
    pieces, _, piece_rows, width = kv.shape
    rows = piece_rows
    blocks = q.shape[0] // rows
    heads = width // HEAD_DIM
    keys_n = pieces * piece_rows
    return pl.pallas_call(
        attend_kernel,
        grid=(blocks,),
        in_specs=[
            pl.BlockSpec((rows, width), lambda i: (i, 0)),
            pl.BlockSpec((pieces, 2, piece_rows, width), lambda i: (0, 0, 0, 0)),
        ],
        out_specs=pl.BlockSpec((1, rows + STAT_ROWS, width), lambda i: (i, 0, 0)),
        out_shape=jax.ShapeDtypeStruct((blocks, rows + STAT_ROWS, width), jnp.bfloat16),
        compiler_params=pltpu.CompilerParams(vmem_limit_bytes=48 * 2**20),
        cost_estimate=pl.CostEstimate(
            flops=4 * q.shape[0] * keys_n * width,
            bytes_accessed=2 * (2 * q.size + kv.size),
            transcendentals=q.shape[0] * keys_n * heads,
        ),
    )(q, kv)


def merge_kernel(parts_ref, out_ref):
    pieces = parts_ref.shape[0]
    rows, width = out_ref.shape
    heads = width // HEAD_DIM
    stats = [
        parts_ref[p, rows : rows + STAT_ROWS, 0:rows].astype(jnp.float32) for p in range(pieces)
    ]
    shifts = [s[0:heads] for s in stats]
    totals = [s[heads : 2 * heads] + s[2 * heads : 3 * heads] for s in stats]
    best = functools.reduce(jnp.maximum, shifts)
    factors = [jnp.exp2(s - best) for s in shifts]
    denom = sum(f * t for f, t in zip(factors, totals))
    weights = jnp.concatenate([f / denom for f in factors], axis=0)
    pad = jnp.zeros((HEAD_DIM - weights.shape[0], rows), jnp.float32)
    weights = jnp.concatenate([weights, pad], axis=0).T
    for h in range(heads):
        cols = slice(h * HEAD_DIM, (h + 1) * HEAD_DIM)
        total = jnp.zeros((rows, HEAD_DIM), jnp.float32)
        for p in range(pieces):
            w = weights[:, p * heads + h : p * heads + h + 1]
            total = total + w * parts_ref[p, 0:rows, cols].astype(jnp.float32)
        out_ref[:, cols] = total.astype(jnp.bfloat16)


def merge(parts):
    pieces, part_rows, width = parts.shape
    return pl.pallas_call(
        merge_kernel,
        out_shape=jax.ShapeDtypeStruct((part_rows - STAT_ROWS, width), jnp.bfloat16),
        in_specs=[pl.BlockSpec(memory_space=pltpu.VMEM)],
        out_specs=pl.BlockSpec(memory_space=pltpu.VMEM),
        compiler_params=pltpu.CompilerParams(vmem_limit_bytes=32 * 2**20),
    )(parts)


HEAD_AXES = ("x", "zl")
KEY_AXES = ("y",)
ROW_AXES = ("zh", "c")
ALL_AXES = ("x", "zl", "y", "zh", "c")


def shards(queries, keys, values):
    rows = queries.shape[0]
    groups = 8
    width = queries.shape[1] // groups
    stacked = jnp.stack([a.reshape(rows, groups, width) for a in (keys, values, queries)])
    stacked = stacked.transpose(2, 0, 1, 3)
    mine = lax.all_to_all(stacked, HEAD_AXES, split_axis=0, concat_axis=0, tiled=True)
    mine = mine.transpose(1, 0, 2, 3).reshape(3, groups * rows, width)
    kv = lax.all_gather(mine[0:2], KEY_AXES, axis=0, tiled=False)
    q = lax.all_gather(mine[2], ROW_AXES, axis=0, tiled=True)
    parts = attend(q, kv)
    parts = lax.all_to_all(parts, ROW_AXES, split_axis=0, concat_axis=0, tiled=True)
    merged = merge(parts).reshape(groups, rows, width)
    spread = lax.all_to_all(merged, HEAD_AXES, split_axis=0, concat_axis=0, tiled=True)
    return spread.transpose(1, 0, 2).reshape(rows, groups * width)


def solution(mesh):
    fine = Mesh(mesh.devices.reshape(4, 2, 8, 4, 2), ALL_AXES)
    placed = P(ALL_AXES, None)
    return jax.shard_map(
        shards, mesh=fine, in_specs=(placed,) * 3, out_specs=placed, check_vma=False
    )
```

```python
import functools
import math

import jax
import jax.numpy as jnp
from jax import lax
from jax.experimental import pallas as pl
from jax.experimental.pallas import tpu as pltpu
from jax.sharding import Mesh, PartitionSpec as P

HEAD_DIM = 128
STAT_ROWS = 16
KEY_CHUNK = 512
EXPONENT = HEAD_DIM**-0.5 * math.log2(math.e)


def head_cols(h):
    return slice(h * HEAD_DIM, (h + 1) * HEAD_DIM)


def attend_kernel(at_ref, q_ref, kv_ref, *refs):
    out_refs, score_refs = refs[:-2], refs[-2:]
    out_rows, width = out_refs[0].shape
    rows = out_rows - STAT_ROWS
    heads = width // HEAD_DIM
    unit_rows = score_refs[0].shape[0]
    slabs, runs, _, run, _ = kv_ref.shape
    keys_n = slabs * runs * run
    chunks = keys_n // KEY_CHUNK
    slab_step = slabs // chunks

    def kv_chunk(which, h, j):
        block = kv_ref[j * slab_step : (j + 1) * slab_step, :, which, :, head_cols(h)]
        return block.reshape(KEY_CHUNK, HEAD_DIM)

    def score_chunk(q, h, j, top):
        s = lax.dot_general(
            q, kv_chunk(0, h, j), (((1,), (1,)), ((), ())), preferred_element_type=jnp.float32
        )
        score_refs[h % 2][:, j * KEY_CHUNK : (j + 1) * KEY_CHUNK] = s
        for t in range(KEY_CHUNK // HEAD_DIM):
            part = s[:, head_cols(t)]
            top = part if top is None else jnp.maximum(top, part)
        return top

    def query(h):
        return jnp.concatenate(
            [q_ref[at_ref[b], :, head_cols(h)] for b in range(len(out_refs))], axis=0
        )

    def shift_of(top):
        best = jnp.max(top, axis=1, keepdims=True) * EXPONENT
        return best.astype(jnp.bfloat16).astype(jnp.float32)

    ones = jnp.ones((KEY_CHUNK, HEAD_DIM), jnp.bfloat16)
    top = None
    q = query(0)
    for j in range(chunks):
        top = score_chunk(q, 0, j, top)
    shift = shift_of(top)
    lane = lax.broadcasted_iota(jnp.int32, (unit_rows, HEAD_DIM), 1)
    stats = jnp.zeros((unit_rows, HEAD_DIM), jnp.float32)
    for h in range(heads):
        more = h + 1 < heads
        top, total = None, None
        if more:
            q = query(h + 1)
        for j in range(chunks):
            if more:
                top = score_chunk(q, h + 1, j, top)
            s = score_refs[h % 2][:, j * KEY_CHUNK : (j + 1) * KEY_CHUNK]
            e = jnp.exp2(s * EXPONENT - shift).astype(jnp.bfloat16)
            v = jnp.concatenate([kv_chunk(1, h, j), ones], axis=1)
            o = jnp.dot(e, v, preferred_element_type=jnp.float32)
            total = o if total is None else total + o
        for b, out_ref in enumerate(out_refs):
            part = total[b * rows : (b + 1) * rows, 0:HEAD_DIM]
            out_ref[0:rows, head_cols(h)] = part.astype(jnp.bfloat16)
        denom = total[:, HEAD_DIM:]
        high = denom.astype(jnp.bfloat16).astype(jnp.float32)
        stats = jnp.where(lane == h, shift, stats)
        stats = jnp.where(lane == heads + h, high, stats)
        stats = jnp.where(lane == 2 * heads + h, denom - high, stats)
        if more:
            shift = shift_of(top)
    flipped = stats.T[0:STAT_ROWS].astype(jnp.bfloat16)
    for b, out_ref in enumerate(out_refs):
        out_ref[rows:, 0:rows] = flipped[:, b * rows : (b + 1) * rows]
        out_ref[rows:, rows:] = jnp.zeros((STAT_ROWS, width - rows), jnp.bfloat16)


def attend(at, q, kv):
    count = at.shape[0]
    _, rows, width = q.shape
    heads = width // HEAD_DIM
    keys_n = kv.size // (2 * width)
    vmem = pl.BlockSpec(memory_space=pltpu.VMEM)
    return pl.pallas_call(
        attend_kernel,
        in_specs=[pl.BlockSpec(memory_space=pltpu.SMEM), vmem, vmem],
        out_specs=[vmem] * count,
        out_shape=[jax.ShapeDtypeStruct((rows + STAT_ROWS, width), jnp.bfloat16)] * count,
        scratch_shapes=[pltpu.VMEM((count * rows, keys_n), jnp.float32)] * 2,
        compiler_params=pltpu.CompilerParams(vmem_limit_bytes=28 * 2**20),
        cost_estimate=pl.CostEstimate(
            flops=4 * count * rows * keys_n * width,
            bytes_accessed=2 * (2 * count * rows * width + kv.size),
            transcendentals=count * rows * keys_n * heads,
        ),
    )(at, q, kv)


def merge_kernel(*refs):
    *part_refs, out_ref = refs
    rows, width = out_ref.shape
    heads = width // HEAD_DIM
    stats = [
        ref[rows : rows + STAT_ROWS, 0:rows].astype(jnp.float32) for ref in part_refs
    ]
    shifts = [s[0:heads] for s in stats]
    totals = [s[heads : 2 * heads] + s[2 * heads : 3 * heads] for s in stats]
    best = functools.reduce(jnp.maximum, shifts)
    factors = [jnp.exp2(s - best) for s in shifts]
    denom = sum(f * t for f, t in zip(factors, totals))
    weights = jnp.concatenate([f / denom for f in factors], axis=0)
    pad = jnp.zeros((HEAD_DIM - weights.shape[0], rows), jnp.float32)
    weights = jnp.concatenate([weights, pad], axis=0).T
    for h in range(heads):
        total = jnp.zeros((rows, HEAD_DIM), jnp.float32)
        for p, ref in enumerate(part_refs):
            w = weights[:, p * heads + h : p * heads + h + 1]
            total = total + w * ref[0:rows, head_cols(h)].astype(jnp.float32)
        out_ref[:, head_cols(h)] = total.astype(jnp.bfloat16)


def merge(parts):
    part_rows, width = parts[0].shape
    return pl.pallas_call(
        merge_kernel,
        out_shape=jax.ShapeDtypeStruct((part_rows - STAT_ROWS, width), jnp.bfloat16),
        in_specs=[pl.BlockSpec(memory_space=pltpu.VMEM)] * len(parts),
        out_specs=pl.BlockSpec(memory_space=pltpu.VMEM),
        compiler_params=pltpu.CompilerParams(vmem_limit_bytes=32 * 2**20),
    )(*parts)


def split_kernel(*refs):
    *in_refs, out_ref = refs
    groups, arrays, rows, width = out_ref.shape
    for g in range(groups):
        for a in range(arrays):
            out_ref[g, a] = in_refs[a][:, g * width : (g + 1) * width]


def split(groups, *arrays):
    rows, columns = arrays[0].shape
    return pl.pallas_call(
        split_kernel,
        out_shape=jax.ShapeDtypeStruct(
            (groups, len(arrays), rows, columns // groups), arrays[0].dtype
        ),
        in_specs=[pl.BlockSpec(memory_space=pltpu.VMEM)] * len(arrays),
        out_specs=pl.BlockSpec(memory_space=pltpu.VMEM),
    )(*arrays)


HEAD_AXES = ("zh", "zl")
KEY_AXES = ("y",)
ROW_AXES = ("x", "c")
ALL_AXES = ("x", "zl", "y", "zh", "c")


def exchange(array, axes):
    return lax.all_to_all(array, axes, split_axis=0, concat_axis=0, tiled=True)


def attend_and_send(q, kv, step):
    chips, cores = lax.axis_size("x"), lax.axis_size("c")
    chip = lax.rem(lax.axis_index("x") + step, chips)
    core = lax.axis_index("c")
    at = jnp.stack([chip * cores + core, chip * cores + (1 - core)]).astype(jnp.int32)
    parts = attend(at, q, kv)
    arrived = []
    for other, part in enumerate(parts):
        if step or other:
            perm = [
                (x * cores + c, (x + step) % chips * cores + (c + other) % cores)
                for x in range(chips)
                for c in range(cores)
            ]
            part = lax.ppermute(part, ROW_AXES, perm)
        arrived.append(part)
    return arrived


def shards(queries, keys, values):
    groups = lax.axis_size(HEAD_AXES)
    blocks = lax.axis_size(ROW_AXES)
    rows, columns = queries.shape
    width = columns // groups
    kv = exchange(split(groups, keys, values), HEAD_AXES)
    kv = lax.all_gather(kv, KEY_AXES, axis=0, tiled=False)
    q = exchange(split(groups, queries), HEAD_AXES).reshape(1, groups * rows, width)
    q = exchange(jnp.broadcast_to(q, (blocks, groups * rows, width)), ROW_AXES)
    parts = []
    for step in (2, 1, 3, 0):
        parts += attend_and_send(q, kv, step)
    merged = merge(parts).reshape(groups, rows, width)
    spread = exchange(merged, HEAD_AXES)
    return spread.transpose(1, 0, 2).reshape(rows, columns)


def solution(mesh):
    fine = Mesh(mesh.devices.reshape(4, 2, 8, 4, 2), ALL_AXES)
    placed = P(ALL_AXES, None)
    return jax.shard_map(
        shards, mesh=fine, in_specs=(placed,) * 3, out_specs=placed, check_vma=False
    )
```

```python
import functools
import math

import jax
import jax.numpy as jnp
from jax import lax
from jax.experimental import pallas as pl
from jax.experimental.pallas import tpu as pltpu
from jax.sharding import Mesh, PartitionSpec as P

HEAD_DIM = 128
STAT_ROWS = 16
KEY_CHUNK = 512
EXPONENT = HEAD_DIM**-0.5 * math.log2(math.e)


def head_cols(h):
    return slice(h * HEAD_DIM, (h + 1) * HEAD_DIM)


def attend_kernel(has_state, q_ref, kv_ref, *refs):
    *refs, held_ref, copied, score_a, score_b = refs
    score_refs = (score_a, score_b)
    if has_state:
        sum_ref, stat_ref, out_ref = refs
    else:
        sums_ref, stats_ref = refs
    blocks, rows, width = q_ref.shape
    heads = width // HEAD_DIM
    unit_rows = score_a.shape[0]
    per_unit = unit_rows // rows
    run = held_ref.shape[2]
    step = KEY_CHUNK // run
    chunks = held_ref.shape[0] // step

    def copy(j):
        part = pl.ds(j * step, step)
        return pltpu.make_async_copy(kv_ref.at[part], held_ref.at[part], copied.at[j])

    def kv_chunk(which, h, j):
        block = held_ref[j * step : (j + 1) * step, which, :, head_cols(h)]
        return block.reshape(KEY_CHUNK, HEAD_DIM)

    def query(i, h):
        block = q_ref[i * per_unit : (i + 1) * per_unit, :, head_cols(h)]
        return block.reshape(unit_rows, HEAD_DIM)

    def score_chunk(q, h, slot, j, top):
        s = lax.dot_general(
            q, kv_chunk(0, h, j), (((1,), (1,)), ((), ())), preferred_element_type=jnp.float32
        )
        score_refs[slot][:, j * KEY_CHUNK : (j + 1) * KEY_CHUNK] = s
        for t in range(KEY_CHUNK // HEAD_DIM):
            part = s[:, head_cols(t)]
            top = part if top is None else jnp.maximum(top, part)
        return top

    def span_of(i):
        return slice(i * unit_rows, (i + 1) * unit_rows)

    def shift_of(top, i, h):
        best = jnp.max(top, axis=1, keepdims=True) * EXPONENT
        shift = best.astype(jnp.bfloat16).astype(jnp.float32)
        if has_state:
            shift = jnp.maximum(shift, stat_ref[span_of(i), h : h + 1])
        return shift

    for j in range(chunks):
        copy(j).start()
    work = [(i, h) for i in range(blocks // per_unit) for h in range(heads)]
    lane = lax.broadcasted_iota(jnp.int32, (unit_rows, HEAD_DIM), 1)
    ones = jnp.ones((KEY_CHUNK, HEAD_DIM), jnp.bfloat16)
    top, stats = None, None
    q = query(*work[0])
    for j in range(chunks):
        copy(j).wait()
        top = score_chunk(q, 0, 0, j, top)
    shift = shift_of(top, 0, 0)
    for n, (i, h) in enumerate(work):
        following = work[n + 1] if n + 1 < len(work) else None
        top, total = None, None
        if following:
            q = query(*following)
        for j in range(chunks):
            if following:
                top = score_chunk(q, following[1], (n + 1) % 2, j, top)
            s = score_refs[n % 2][:, j * KEY_CHUNK : (j + 1) * KEY_CHUNK]
            e = jnp.exp2(s * EXPONENT - shift).astype(jnp.bfloat16)
            v = jnp.concatenate([kv_chunk(1, h, j), ones], axis=1)
            o = jnp.dot(e, v, preferred_element_type=jnp.float32)
            total = o if total is None else total + o
        sums, denom = total[:, 0:HEAD_DIM], total[:, HEAD_DIM:]
        span = span_of(i)
        if h == 0:
            stats = jnp.zeros((unit_rows, HEAD_DIM), jnp.float32)
        stats = jnp.where(lane == h, shift, stats)
        if has_state:
            factor = jnp.exp2(stat_ref[span, h : h + 1] - shift)
            sums = sums + factor * sum_ref[span, head_cols(h)]
            denom = denom + factor * stat_ref[span, heads + h : heads + h + 1]
            for b in range(per_unit):
                part = sums[b * rows : (b + 1) * rows].astype(jnp.bfloat16)
                out_ref[i * per_unit + b, 0:rows, head_cols(h)] = part
            high = denom.astype(jnp.bfloat16).astype(jnp.float32)
            stats = jnp.where(lane == heads + h, high, stats)
            stats = jnp.where(lane == 2 * heads + h, denom - high, stats)
        else:
            sums_ref[span, head_cols(h)] = sums
            stats = jnp.where(lane == heads + h, denom, stats)
        if h + 1 == heads:
            if has_state:
                flipped = stats.T[0:STAT_ROWS].astype(jnp.bfloat16)
                blank = jnp.zeros((STAT_ROWS, width - rows), jnp.bfloat16)
                for b in range(per_unit):
                    block = i * per_unit + b
                    out_ref[block, rows:, 0:rows] = flipped[:, b * rows : (b + 1) * rows]
                    out_ref[block, rows:, rows:] = blank
            else:
                stats_ref[span, :] = stats
        if following:
            shift = shift_of(top, *following)


def attend(q, kv, state=None):
    blocks, rows, width = q.shape
    heads = width // HEAD_DIM
    keys_n = kv.shape[0] * kv.shape[2]
    vmem = pl.BlockSpec(memory_space=pltpu.VMEM)
    if state:
        out_shape = jax.ShapeDtypeStruct((blocks, rows + STAT_ROWS, width), jnp.bfloat16)
        out_specs = vmem
    else:
        out_shape = [
            jax.ShapeDtypeStruct((blocks * rows, width), jnp.float32),
            jax.ShapeDtypeStruct((blocks * rows, HEAD_DIM), jnp.float32),
        ]
        out_specs = [vmem, vmem]
    state = state or []
    unit_rows = 2 * rows
    return pl.pallas_call(
        functools.partial(attend_kernel, bool(state)),
        in_specs=[vmem, pl.BlockSpec(memory_space=pl.ANY)] + [vmem] * len(state),
        out_specs=out_specs,
        out_shape=out_shape,
        scratch_shapes=[
            pltpu.VMEM(kv.shape, kv.dtype),
            pltpu.SemaphoreType.DMA((keys_n // KEY_CHUNK,)),
            pltpu.VMEM((unit_rows, keys_n), jnp.float32),
            pltpu.VMEM((unit_rows, keys_n), jnp.float32),
        ],
        compiler_params=pltpu.CompilerParams(vmem_limit_bytes=36 * 2**20),
        cost_estimate=pl.CostEstimate(
            flops=4 * blocks * rows * keys_n * width,
            bytes_accessed=4 * (blocks * rows * width + keys_n * width),
            transcendentals=blocks * rows * keys_n * heads,
        ),
    )(q, kv, *state)


def merge_kernel(parts_ref, out_ref):
    pieces = parts_ref.shape[0]
    rows, width = out_ref.shape
    heads = width // HEAD_DIM
    stats = [
        parts_ref[p, rows : rows + STAT_ROWS, 0:rows].astype(jnp.float32) for p in range(pieces)
    ]
    shifts = [s[0:heads] for s in stats]
    totals = [s[heads : 2 * heads] + s[2 * heads : 3 * heads] for s in stats]
    best = functools.reduce(jnp.maximum, shifts)
    factors = [jnp.exp2(s - best) for s in shifts]
    denom = sum(f * t for f, t in zip(factors, totals))
    weights = jnp.concatenate([f / denom for f in factors], axis=0)
    pad = jnp.zeros((HEAD_DIM - weights.shape[0], rows), jnp.float32)
    weights = jnp.concatenate([weights, pad], axis=0).T
    for h in range(heads):
        total = jnp.zeros((rows, HEAD_DIM), jnp.float32)
        for p in range(pieces):
            w = weights[:, p * heads + h : p * heads + h + 1]
            total = total + w * parts_ref[p, 0:rows, head_cols(h)].astype(jnp.float32)
        out_ref[:, head_cols(h)] = total.astype(jnp.bfloat16)


def merge(parts):
    pieces, part_rows, width = parts.shape
    return pl.pallas_call(
        merge_kernel,
        out_shape=jax.ShapeDtypeStruct((part_rows - STAT_ROWS, width), jnp.bfloat16),
        in_specs=[pl.BlockSpec(memory_space=pltpu.VMEM)],
        out_specs=pl.BlockSpec(memory_space=pltpu.VMEM),
        compiler_params=pltpu.CompilerParams(vmem_limit_bytes=32 * 2**20),
    )(parts)


def split_kernel(*refs):
    *in_refs, out_ref = refs
    groups, arrays, rows, width = out_ref.shape
    for g in range(groups):
        for a in range(arrays):
            out_ref[g, a] = in_refs[a][:, g * width : (g + 1) * width]


def split(groups, *arrays):
    rows, columns = arrays[0].shape
    return pl.pallas_call(
        split_kernel,
        out_shape=jax.ShapeDtypeStruct(
            (groups, len(arrays), rows, columns // groups), arrays[0].dtype
        ),
        in_specs=[pl.BlockSpec(memory_space=pltpu.VMEM)] * len(arrays),
        out_specs=pl.BlockSpec(memory_space=pltpu.VMEM),
    )(*arrays)


HEAD_AXES = ("zh", "zl")
KEY_AXES = ("y",)
ROW_AXES = ("x",)
ALL_AXES = ("x", "zl", "y", "zh", "c")


def exchange(array, axes):
    return lax.all_to_all(array, axes, split_axis=0, concat_axis=0, tiled=True)


def shards(queries, keys, values):
    groups = lax.axis_size(HEAD_AXES)
    blocks = lax.axis_size(ROW_AXES)
    rows, columns = queries.shape
    width = columns // groups
    kv = exchange(split(groups, keys, values), HEAD_AXES)
    kv = lax.all_gather(kv, KEY_AXES, axis=0, tiled=True)
    q = exchange(split(groups, queries), HEAD_AXES).reshape(1, groups * rows, width)
    q = exchange(jnp.broadcast_to(q, (blocks, groups * rows, width)), ROW_AXES)
    kv, q = lax.optimization_barrier((kv, q))
    other_kv = lax.ppermute(kv, "c", [(0, 1), (1, 0)])
    parts = attend(q, other_kv, attend(q, kv))
    merged = merge(exchange(parts, ROW_AXES)).reshape(groups, rows, width)
    spread = exchange(merged, HEAD_AXES)
    return spread.transpose(1, 0, 2).reshape(rows, columns)


def solution(mesh):
    fine = Mesh(mesh.devices.reshape(4, 2, 8, 4, 2), ALL_AXES)
    placed = P(ALL_AXES, None)
    return jax.shard_map(
        shards, mesh=fine, in_specs=(placed,) * 3, out_specs=placed, check_vma=False
    )
```

```python
import functools
import math

import jax
import jax.numpy as jnp
from jax import lax
from jax.experimental import pallas as pl
from jax.experimental.pallas import tpu as pltpu
from jax.sharding import Mesh, PartitionSpec as P

HEAD_DIM = 128
STAT_ROWS = 16
KEY_CHUNK = 512
EXPONENT = HEAD_DIM**-0.5 * math.log2(math.e)


def head_cols(h):
    return slice(h * HEAD_DIM, (h + 1) * HEAD_DIM)


def attend_kernel(has_state, q_ref, kv_ref, *refs):
    *refs, held_ref, copied, score_a, score_b = refs
    score_refs = (score_a, score_b)
    if has_state:
        sum_ref, stat_ref, out_ref = refs
    else:
        sums_ref, stats_ref = refs
    blocks, rows, width = q_ref.shape
    heads = width // HEAD_DIM
    unit_rows = score_a.shape[0]
    per_unit = unit_rows // rows
    run = held_ref.shape[2]
    step = KEY_CHUNK // run
    chunks = held_ref.shape[0] // step

    def copy(j):
        part = pl.ds(j * step, step)
        return pltpu.make_async_copy(kv_ref.at[part], held_ref.at[part], copied.at[j])

    def kv_chunk(which, h, j):
        block = held_ref[j * step : (j + 1) * step, which, :, head_cols(h)]
        return block.reshape(KEY_CHUNK, HEAD_DIM)

    def query(i, h):
        block = q_ref[i * per_unit : (i + 1) * per_unit, :, head_cols(h)]
        return block.reshape(unit_rows, HEAD_DIM)

    def score_chunk(q, h, slot, j, top):
        s = lax.dot_general(
            q, kv_chunk(0, h, j), (((1,), (1,)), ((), ())), preferred_element_type=jnp.float32
        )
        score_refs[slot][:, j * KEY_CHUNK : (j + 1) * KEY_CHUNK] = s
        for t in range(KEY_CHUNK // HEAD_DIM):
            part = s[:, head_cols(t)]
            top = part if top is None else jnp.maximum(top, part)
        return top

    def span_of(i):
        return slice(i * unit_rows, (i + 1) * unit_rows)

    def shift_of(top, i, h):
        best = jnp.max(top, axis=1, keepdims=True) * EXPONENT
        shift = best.astype(jnp.bfloat16).astype(jnp.float32)
        if has_state:
            shift = jnp.maximum(shift, stat_ref[span_of(i), h : h + 1])
        return shift

    for j in range(chunks):
        copy(j).start()
    work = [(i, h) for i in range(blocks // per_unit) for h in range(heads)]
    lane = lax.broadcasted_iota(jnp.int32, (unit_rows, HEAD_DIM), 1)
    ones = jnp.ones((KEY_CHUNK, HEAD_DIM), jnp.bfloat16)
    top, stats = None, None
    q = query(*work[0])
    for j in range(chunks):
        copy(j).wait()
        top = score_chunk(q, 0, 0, j, top)
    shift = shift_of(top, 0, 0)
    for n, (i, h) in enumerate(work):
        following = work[n + 1] if n + 1 < len(work) else None
        top, total = None, None
        if following:
            q = query(*following)
        for j in range(chunks):
            if following:
                top = score_chunk(q, following[1], (n + 1) % 2, j, top)
            s = score_refs[n % 2][:, j * KEY_CHUNK : (j + 1) * KEY_CHUNK]
            e = jnp.exp2(s * EXPONENT - shift).astype(jnp.bfloat16)
            v = jnp.concatenate([kv_chunk(1, h, j), ones], axis=1)
            o = jnp.dot(e, v, preferred_element_type=jnp.float32)
            total = o if total is None else total + o
        sums, denom = total[:, 0:HEAD_DIM], total[:, HEAD_DIM:]
        span = span_of(i)
        if h == 0:
            stats = jnp.zeros((unit_rows, HEAD_DIM), jnp.float32)
        stats = jnp.where(lane == h, shift, stats)
        if has_state:
            factor = jnp.exp2(stat_ref[span, h : h + 1] - shift)
            sums = sums + factor * sum_ref[span, head_cols(h)]
            denom = denom + factor * stat_ref[span, heads + h : heads + h + 1]
            for b in range(per_unit):
                part = sums[b * rows : (b + 1) * rows].astype(jnp.bfloat16)
                out_ref[i * per_unit + b, 0:rows, head_cols(h)] = part
            high = denom.astype(jnp.bfloat16).astype(jnp.float32)
            stats = jnp.where(lane == heads + h, high, stats)
            stats = jnp.where(lane == 2 * heads + h, denom - high, stats)
        else:
            sums_ref[span, head_cols(h)] = sums
            stats = jnp.where(lane == heads + h, denom, stats)
        if h + 1 == heads:
            if has_state:
                flipped = stats.T[0:STAT_ROWS].astype(jnp.bfloat16)
                blank = jnp.zeros((STAT_ROWS, width - rows), jnp.bfloat16)
                for b in range(per_unit):
                    block = i * per_unit + b
                    out_ref[block, rows:, 0:rows] = flipped[:, b * rows : (b + 1) * rows]
                    out_ref[block, rows:, rows:] = blank
            else:
                stats_ref[span, :] = stats
        if following:
            shift = shift_of(top, *following)


def attend(q, kv, state=None):
    blocks, rows, width = q.shape
    heads = width // HEAD_DIM
    keys_n = kv.shape[0] * kv.shape[2]
    vmem = pl.BlockSpec(memory_space=pltpu.VMEM)
    if state:
        out_shape = jax.ShapeDtypeStruct((blocks, rows + STAT_ROWS, width), jnp.bfloat16)
        out_specs = vmem
    else:
        out_shape = [
            jax.ShapeDtypeStruct((blocks * rows, width), jnp.float32),
            jax.ShapeDtypeStruct((blocks * rows, HEAD_DIM), jnp.float32),
        ]
        out_specs = [vmem, vmem]
    state = state or []
    unit_rows = 2 * rows
    return pl.pallas_call(
        functools.partial(attend_kernel, bool(state)),
        in_specs=[vmem, pl.BlockSpec(memory_space=pl.ANY if state else pltpu.HBM)] + [vmem] * len(state),
        out_specs=out_specs,
        out_shape=out_shape,
        scratch_shapes=[
            pltpu.VMEM(kv.shape, kv.dtype),
            pltpu.SemaphoreType.DMA((keys_n // KEY_CHUNK,)),
            pltpu.VMEM((unit_rows, keys_n), jnp.float32),
            pltpu.VMEM((unit_rows, keys_n), jnp.float32),
        ],
        compiler_params=pltpu.CompilerParams(vmem_limit_bytes=36 * 2**20),
        cost_estimate=pl.CostEstimate(
            flops=4 * blocks * rows * keys_n * width,
            bytes_accessed=4 * (blocks * rows * width + keys_n * width),
            transcendentals=blocks * rows * keys_n * heads,
        ),
    )(q, kv, *state)


def merge_kernel(parts_ref, out_ref):
    pieces = parts_ref.shape[0]
    rows, width = out_ref.shape
    heads = width // HEAD_DIM
    stats = [
        parts_ref[p, rows : rows + STAT_ROWS, 0:rows].astype(jnp.float32) for p in range(pieces)
    ]
    shifts = [s[0:heads] for s in stats]
    totals = [s[heads : 2 * heads] + s[2 * heads : 3 * heads] for s in stats]
    best = functools.reduce(jnp.maximum, shifts)
    factors = [jnp.exp2(s - best) for s in shifts]
    denom = sum(f * t for f, t in zip(factors, totals))
    weights = jnp.concatenate([f / denom for f in factors], axis=0)
    pad = jnp.zeros((HEAD_DIM - weights.shape[0], rows), jnp.float32)
    weights = jnp.concatenate([weights, pad], axis=0).T
    for h in range(heads):
        total = jnp.zeros((rows, HEAD_DIM), jnp.float32)
        for p in range(pieces):
            w = weights[:, p * heads + h : p * heads + h + 1]
            total = total + w * parts_ref[p, 0:rows, head_cols(h)].astype(jnp.float32)
        out_ref[:, head_cols(h)] = total.astype(jnp.bfloat16)


def merge(parts):
    pieces, part_rows, width = parts.shape
    return pl.pallas_call(
        merge_kernel,
        out_shape=jax.ShapeDtypeStruct((part_rows - STAT_ROWS, width), jnp.bfloat16),
        in_specs=[pl.BlockSpec(memory_space=pltpu.VMEM)],
        out_specs=pl.BlockSpec(memory_space=pltpu.VMEM),
        compiler_params=pltpu.CompilerParams(vmem_limit_bytes=32 * 2**20),
    )(parts)


def split_kernel(*refs):
    *in_refs, out_ref = refs
    groups, arrays, rows, width = out_ref.shape
    for g in range(groups):
        for a in range(arrays):
            out_ref[g, a] = in_refs[a][:, g * width : (g + 1) * width]


def split(groups, *arrays):
    rows, columns = arrays[0].shape
    return pl.pallas_call(
        split_kernel,
        out_shape=jax.ShapeDtypeStruct(
            (groups, len(arrays), rows, columns // groups), arrays[0].dtype
        ),
        in_specs=[pl.BlockSpec(memory_space=pltpu.VMEM)] * len(arrays),
        out_specs=pl.BlockSpec(memory_space=pltpu.VMEM),
    )(*arrays)


HEAD_AXES = ("x", "zl")
KEY_AXES = ("y",)
ROW_AXES = ("zh",)
ALL_AXES = ("x", "zl", "y", "zh", "c")


def exchange(array, axes):
    return lax.all_to_all(array, axes, split_axis=0, concat_axis=0, tiled=True)


def shards(queries, keys, values):
    groups = lax.axis_size(HEAD_AXES)
    blocks = lax.axis_size(ROW_AXES)
    rows, columns = queries.shape
    width = columns // groups
    kv = exchange(split(groups, keys, values), HEAD_AXES)
    kv = lax.all_gather(kv, KEY_AXES, axis=0, tiled=True)
    q = exchange(split(groups, queries), HEAD_AXES).reshape(1, groups * rows, width)
    q = exchange(jnp.broadcast_to(q, (blocks, groups * rows, width)), ROW_AXES)
    kv, q = lax.optimization_barrier((kv, q))
    other_kv = lax.ppermute(kv, "c", [(0, 1), (1, 0)])
    parts = attend(q, other_kv, attend(q, kv))
    merged = merge(exchange(parts, ROW_AXES)).reshape(groups, rows, width)
    spread = exchange(merged, HEAD_AXES)
    return spread.transpose(1, 0, 2).reshape(rows, columns)


def solution(mesh):
    fine = Mesh(mesh.devices.reshape(4, 2, 8, 4, 2), ALL_AXES)
    placed = P(ALL_AXES, None)
    return jax.shard_map(
        shards, mesh=fine, in_specs=(placed,) * 3, out_specs=placed, check_vma=False
    )
```

```python
import functools
import math

import jax
import jax.numpy as jnp
from jax import lax
from jax.experimental import pallas as pl
from jax.experimental.pallas import tpu as pltpu
from jax.sharding import Mesh, PartitionSpec as P

HEAD_DIM = 128
STAT_ROWS = 16
KEY_CHUNK = 512
EXPONENT = HEAD_DIM**-0.5 * math.log2(math.e)


def head_cols(h):
    return slice(h * HEAD_DIM, (h + 1) * HEAD_DIM)


def attend_kernel(at_ref, q_ref, kv_ref, *refs):
    *out_refs, held_ref, copied, score_a, score_b = refs
    score_refs = (score_a, score_b)
    blocks, rows, width = q_ref.shape
    heads = width // HEAD_DIM
    unit_rows = score_a.shape[0]
    per_unit = unit_rows // rows
    run = held_ref.shape[2]
    step = KEY_CHUNK // run
    chunks = held_ref.shape[0] // step

    def copy(which, j):
        part = pl.ds(j * step, step)
        return pltpu.make_async_copy(
            kv_ref.at[part, which], held_ref.at[part, which], copied.at[which, j]
        )

    def kv_chunk(which, h, j):
        block = held_ref[j * step : (j + 1) * step, which, :, head_cols(h)]
        return block.reshape(KEY_CHUNK, HEAD_DIM)

    def query(i, h):
        parts = [q_ref[at_ref[i * per_unit + b], :, head_cols(h)] for b in range(per_unit)]
        return jnp.concatenate(parts, axis=0)

    def cols_of(j):
        return slice(j * KEY_CHUNK, (j + 1) * KEY_CHUNK)

    def score_chunk(q, h, slot, j, top):
        s = lax.dot_general(
            q, kv_chunk(0, h, j), (((1,), (1,)), ((), ())), preferred_element_type=jnp.float32
        )
        score_refs[slot][:, cols_of(j)] = s
        for t in range(KEY_CHUNK // HEAD_DIM):
            part = s[:, head_cols(t)]
            top = part if top is None else jnp.maximum(top, part)
        return top

    def shift_of(top):
        best = jnp.max(top, axis=1, keepdims=True) * EXPONENT
        return best.astype(jnp.bfloat16).astype(jnp.float32)

    for which in range(2):
        for j in range(chunks):
            copy(which, j).start()
    work = [(i, h) for i in range(blocks // per_unit) for h in range(heads)]
    lane = lax.broadcasted_iota(jnp.int32, (unit_rows, HEAD_DIM), 1)
    ones = jnp.ones((KEY_CHUNK, HEAD_DIM), jnp.bfloat16)
    top, stats = None, None
    q = query(*work[0])
    for j in range(chunks):
        copy(0, j).wait()
        top = score_chunk(q, 0, 0, j, top)
    shift = shift_of(top)
    for n, (i, h) in enumerate(work):
        following = work[n + 1] if n + 1 < len(work) else None
        top, total = None, None
        if following:
            q = query(*following)
        for j in range(chunks):
            if following:
                top = score_chunk(q, following[1], (n + 1) % 2, j, top)
            s = score_refs[n % 2][:, cols_of(j)]
            e = jnp.exp2(s * EXPONENT - shift).astype(jnp.bfloat16)
            if n == 0:
                copy(1, j).wait()
            v = jnp.concatenate([kv_chunk(1, h, j), ones], axis=1)
            o = jnp.dot(e, v, preferred_element_type=jnp.float32)
            total = o if total is None else total + o
        sums, denom = total[:, 0:HEAD_DIM], total[:, HEAD_DIM:]
        for b in range(per_unit):
            part = sums[b * rows : (b + 1) * rows].astype(jnp.bfloat16)
            out_refs[i * per_unit + b][0:rows, head_cols(h)] = part
        if h == 0:
            stats = jnp.zeros((unit_rows, HEAD_DIM), jnp.float32)
        high = denom.astype(jnp.bfloat16).astype(jnp.float32)
        stats = jnp.where(lane == h, shift, stats)
        stats = jnp.where(lane == heads + h, high, stats)
        stats = jnp.where(lane == 2 * heads + h, denom - high, stats)
        if h + 1 == heads:
            flipped = stats.T[0:STAT_ROWS].astype(jnp.bfloat16)
            blank = jnp.zeros((STAT_ROWS, width - rows), jnp.bfloat16)
            for b in range(per_unit):
                out_ref = out_refs[i * per_unit + b]
                out_ref[rows:, 0:rows] = flipped[:, b * rows : (b + 1) * rows]
                out_ref[rows:, rows:] = blank
        if following:
            shift = shift_of(top)


def attend(at, q, kv):
    blocks, rows, width = q.shape
    heads = width // HEAD_DIM
    keys_n = kv.shape[0] * kv.shape[2]
    vmem = pl.BlockSpec(memory_space=pltpu.VMEM)
    unit_rows = 2 * rows
    return pl.pallas_call(
        attend_kernel,
        in_specs=[
            pl.BlockSpec(memory_space=pltpu.SMEM),
            vmem,
            pl.BlockSpec(memory_space=pl.ANY),
        ],
        out_specs=[vmem] * blocks,
        out_shape=[jax.ShapeDtypeStruct((rows + STAT_ROWS, width), jnp.bfloat16)] * blocks,
        scratch_shapes=[
            pltpu.VMEM(kv.shape, kv.dtype),
            pltpu.SemaphoreType.DMA((2, keys_n // KEY_CHUNK)),
            pltpu.VMEM((unit_rows, keys_n), jnp.float32),
            pltpu.VMEM((unit_rows, keys_n), jnp.float32),
        ],
        compiler_params=pltpu.CompilerParams(vmem_limit_bytes=56 * 2**20),
        cost_estimate=pl.CostEstimate(
            flops=4 * blocks * rows * keys_n * width,
            bytes_accessed=4 * (blocks * rows * width + keys_n * width),
            transcendentals=blocks * rows * keys_n * heads,
        ),
    )(at, q, kv)


def merge_kernel(*refs):
    *part_refs, out_ref = refs
    rows, width = out_ref.shape
    heads = width // HEAD_DIM
    stats = [
        ref[rows : rows + STAT_ROWS, 0:rows].astype(jnp.float32) for ref in part_refs
    ]
    shifts = [s[0:heads] for s in stats]
    totals = [s[heads : 2 * heads] + s[2 * heads : 3 * heads] for s in stats]
    best = functools.reduce(jnp.maximum, shifts)
    factors = [jnp.exp2(s - best) for s in shifts]
    denom = sum(f * t for f, t in zip(factors, totals))
    weights = jnp.concatenate([f / denom for f in factors], axis=0)
    pad = jnp.zeros((HEAD_DIM - weights.shape[0], rows), jnp.float32)
    weights = jnp.concatenate([weights, pad], axis=0).T
    for h in range(heads):
        total = jnp.zeros((rows, HEAD_DIM), jnp.float32)
        for p, ref in enumerate(part_refs):
            w = weights[:, p * heads + h : p * heads + h + 1]
            total = total + w * ref[0:rows, head_cols(h)].astype(jnp.float32)
        out_ref[:, head_cols(h)] = total.astype(jnp.bfloat16)


def merge(parts):
    part_rows, width = parts[0].shape
    return pl.pallas_call(
        merge_kernel,
        out_shape=jax.ShapeDtypeStruct((part_rows - STAT_ROWS, width), jnp.bfloat16),
        in_specs=[pl.BlockSpec(memory_space=pltpu.VMEM)] * len(parts),
        out_specs=pl.BlockSpec(memory_space=pltpu.VMEM),
        compiler_params=pltpu.CompilerParams(vmem_limit_bytes=32 * 2**20),
    )(*parts)


def split_kernel(*refs):
    *in_refs, out_ref = refs
    groups, arrays, rows, width = out_ref.shape
    for g in range(groups):
        for a in range(arrays):
            out_ref[g, a] = in_refs[a][:, g * width : (g + 1) * width]


def split(groups, *arrays):
    rows, columns = arrays[0].shape
    return pl.pallas_call(
        split_kernel,
        out_shape=jax.ShapeDtypeStruct(
            (groups, len(arrays), rows, columns // groups), arrays[0].dtype
        ),
        in_specs=[pl.BlockSpec(memory_space=pltpu.VMEM)] * len(arrays),
        out_specs=pl.BlockSpec(memory_space=pltpu.VMEM),
    )(*arrays)


HEAD_AXES = ("zh", "zl")
KEY_AXES = ("y", "c")
ROW_AXES = ("x",)
ALL_AXES = ("x", "zl", "y", "zh", "c")


def exchange(array, axes):
    return lax.all_to_all(array, axes, split_axis=0, concat_axis=0, tiled=True)


def shards(queries, keys, values):
    groups = lax.axis_size(HEAD_AXES)
    blocks = lax.axis_size(ROW_AXES)
    rows, columns = queries.shape
    width = columns // groups
    kv = exchange(split(groups, keys, values), HEAD_AXES)
    kv = lax.all_gather(kv, KEY_AXES, axis=0, tiled=True)
    q = exchange(split(groups, queries), HEAD_AXES).reshape(1, groups * rows, width)
    q = exchange(jnp.broadcast_to(q, (blocks, groups * rows, width)), ROW_AXES)
    steps = (2, 1, 3, 0)
    place = lax.axis_index(ROW_AXES)
    at = jnp.stack([lax.rem(place + step, blocks) for step in steps]).astype(jnp.int32)
    parts = [
        lax.ppermute(part, ROW_AXES, [(i, (i + step) % blocks) for i in range(blocks)])
        if step
        else part
        for step, part in zip(steps, attend(at, q, kv))
    ]
    merged = merge(parts).reshape(groups, rows, width)
    spread = exchange(merged, HEAD_AXES)
    return spread.transpose(1, 0, 2).reshape(rows, columns)


def solution(mesh):
    fine = Mesh(mesh.devices.reshape(4, 2, 8, 4, 2), ALL_AXES)
    placed = P(ALL_AXES, None)
    return jax.shard_map(
        shards, mesh=fine, in_specs=(placed,) * 3, out_specs=placed, check_vma=False
    )
```

```python
import functools
import math

import jax
import jax.numpy as jnp
from jax import lax
from jax.experimental import pallas as pl
from jax.experimental.pallas import tpu as pltpu
from jax.sharding import Mesh, PartitionSpec as P

HEAD_DIM = 128
STAT_ROWS = 16
KEY_CHUNK = 512
EXPONENT = HEAD_DIM**-0.5 * math.log2(math.e)


def head_cols(h):
    return slice(h * HEAD_DIM, (h + 1) * HEAD_DIM)


def attend_kernel(q_ref, kv_ref, out_ref, held_ref, copied, score_a, score_b):
    score_refs = (score_a, score_b)
    blocks, rows, width = q_ref.shape
    heads = width // HEAD_DIM
    unit_rows = score_a.shape[0]
    per_unit = unit_rows // rows
    units = blocks // per_unit
    run = held_ref.shape[2]
    step = KEY_CHUNK // run
    chunks = held_ref.shape[0] // (2 * step)

    def copy(j):
        part = pl.ds(j * step, step)
        return pltpu.make_async_copy(kv_ref.at[part], held_ref.at[part], copied.at[j])

    def kv_chunk(which, h, j):
        block = held_ref[j * step : (j + 1) * step, which, :, head_cols(h)]
        return block.reshape(KEY_CHUNK, HEAD_DIM)

    def query(i, h):
        block = q_ref[pl.ds(i * per_unit, per_unit), :, head_cols(h)]
        return block.reshape(unit_rows, HEAD_DIM)

    def cols_of(j):
        return slice(j * KEY_CHUNK, (j + 1) * KEY_CHUNK)

    def score_chunk(q, h, half, slot, j, top):
        k = kv_chunk(0, h, half * chunks + j)
        s = lax.dot_general(q, k, (((1,), (1,)), ((), ())), preferred_element_type=jnp.float32)
        score_refs[slot][:, cols_of(j)] = s
        for t in range(KEY_CHUNK // HEAD_DIM):
            part = s[:, head_cols(t)]
            top = part if top is None else jnp.maximum(top, part)
        return top

    def shift_of(top):
        best = jnp.max(top, axis=1, keepdims=True) * EXPONENT
        return best.astype(jnp.bfloat16).astype(jnp.float32)

    for j in range(2 * chunks):
        copy(j).start()
    ones = jnp.ones((KEY_CHUNK, HEAD_DIM), jnp.bfloat16)
    order = [(half, h) for half in range(2) for h in range(heads)]
    top = None
    q = query(0, 0)
    for j in range(chunks):
        copy(j).wait()
        top = score_chunk(q, 0, 0, 0, j, top)

    def rows_step(i, shift):
        lane = lax.broadcasted_iota(jnp.int32, (unit_rows, HEAD_DIM), 1)
        stats = jnp.zeros((unit_rows, HEAD_DIM), jnp.float32)
        held = {}
        for n, (half, h) in enumerate(order):
            if n == heads - 1:

                @pl.when(i == 0)
                def _():
                    for j in range(chunks, 2 * chunks):
                        copy(j).wait()

            wraps = n + 1 == len(order)
            next_half, next_h = order[(n + 1) % len(order)]
            q = query(jnp.minimum(i + 1, units - 1) if wraps else i, next_h)
            if half:
                shift_before, total_before = held[h]
                shift = jnp.maximum(shift, shift_before)
            top, total = None, None
            for j in range(chunks):
                top = score_chunk(q, next_h, next_half, (n + 1) % 2, j, top)
                s = score_refs[n % 2][:, cols_of(j)]
                e = jnp.exp2(s * EXPONENT - shift).astype(jnp.bfloat16)
                v = jnp.concatenate([kv_chunk(1, h, half * chunks + j), ones], axis=1)
                o = jnp.dot(e, v, preferred_element_type=jnp.float32)
                total = o if total is None else total + o
            if half:
                total = total + jnp.exp2(shift_before - shift) * total_before
                for b in range(per_unit):
                    part = total[b * rows : (b + 1) * rows, 0:HEAD_DIM].astype(jnp.bfloat16)
                    out_ref[i * per_unit + b, 0:rows, head_cols(h)] = part
                denom = total[:, HEAD_DIM:]
                high = denom.astype(jnp.bfloat16).astype(jnp.float32)
                stats = jnp.where(lane == h, shift, stats)
                stats = jnp.where(lane == heads + h, high, stats)
                stats = jnp.where(lane == 2 * heads + h, denom - high, stats)
            else:
                held[h] = shift, total
            shift = shift_of(top)
        flipped = stats.T[0:STAT_ROWS].astype(jnp.bfloat16)
        blank = jnp.zeros((STAT_ROWS, width - rows), jnp.bfloat16)
        for b in range(per_unit):
            block = i * per_unit + b
            out_ref[block, rows:, 0:rows] = flipped[:, b * rows : (b + 1) * rows]
            out_ref[block, rows:, rows:] = blank
        return shift

    lax.fori_loop(0, units, rows_step, shift_of(top))


def attend(q, kv):
    blocks, rows, width = q.shape
    heads = width // HEAD_DIM
    keys_n = kv.shape[0] * kv.shape[2]
    vmem = pl.BlockSpec(memory_space=pltpu.VMEM)
    unit_rows = 2 * rows
    return pl.pallas_call(
        attend_kernel,
        in_specs=[vmem, pl.BlockSpec(memory_space=pl.ANY)],
        out_specs=vmem,
        out_shape=jax.ShapeDtypeStruct((blocks, rows + STAT_ROWS, width), jnp.bfloat16),
        scratch_shapes=[
            pltpu.VMEM(kv.shape, kv.dtype),
            pltpu.SemaphoreType.DMA((keys_n // KEY_CHUNK,)),
            pltpu.VMEM((unit_rows, keys_n // 2), jnp.float32),
            pltpu.VMEM((unit_rows, keys_n // 2), jnp.float32),
        ],
        compiler_params=pltpu.CompilerParams(vmem_limit_bytes=56 * 2**20),
        cost_estimate=pl.CostEstimate(
            flops=4 * blocks * rows * keys_n * width,
            bytes_accessed=4 * (blocks * rows * width + keys_n * width),
            transcendentals=blocks * rows * keys_n * heads,
        ),
    )(q, kv)


def merge_kernel(parts_ref, out_ref):
    pieces = parts_ref.shape[0]
    rows, width = out_ref.shape
    heads = width // HEAD_DIM
    stats = [
        parts_ref[p, rows : rows + STAT_ROWS, 0:rows].astype(jnp.float32) for p in range(pieces)
    ]
    shifts = [s[0:heads] for s in stats]
    totals = [s[heads : 2 * heads] + s[2 * heads : 3 * heads] for s in stats]
    best = functools.reduce(jnp.maximum, shifts)
    factors = [jnp.exp2(s - best) for s in shifts]
    denom = sum(f * t for f, t in zip(factors, totals))
    weights = jnp.concatenate([f / denom for f in factors], axis=0)
    pad = jnp.zeros((HEAD_DIM - weights.shape[0], rows), jnp.float32)
    weights = jnp.concatenate([weights, pad], axis=0).T
    for h in range(heads):
        total = jnp.zeros((rows, HEAD_DIM), jnp.float32)
        for p in range(pieces):
            w = weights[:, p * heads + h : p * heads + h + 1]
            total = total + w * parts_ref[p, 0:rows, head_cols(h)].astype(jnp.float32)
        out_ref[:, head_cols(h)] = total.astype(jnp.bfloat16)


def merge(parts):
    pieces, part_rows, width = parts.shape
    return pl.pallas_call(
        merge_kernel,
        out_shape=jax.ShapeDtypeStruct((part_rows - STAT_ROWS, width), jnp.bfloat16),
        in_specs=[pl.BlockSpec(memory_space=pltpu.VMEM)],
        out_specs=pl.BlockSpec(memory_space=pltpu.VMEM),
        compiler_params=pltpu.CompilerParams(vmem_limit_bytes=32 * 2**20),
    )(parts)


def split_kernel(*refs):
    *in_refs, out_ref = refs
    groups, arrays, rows, width = out_ref.shape
    for g in range(groups):
        for a in range(arrays):
            out_ref[g, a] = in_refs[a][:, g * width : (g + 1) * width]


def split(groups, *arrays):
    rows, columns = arrays[0].shape
    return pl.pallas_call(
        split_kernel,
        out_shape=jax.ShapeDtypeStruct(
            (groups, len(arrays), rows, columns // groups), arrays[0].dtype
        ),
        in_specs=[pl.BlockSpec(memory_space=pltpu.VMEM)] * len(arrays),
        out_specs=pl.BlockSpec(memory_space=pltpu.VMEM),
    )(*arrays)


HEAD_AXES = ("zh", "zl")
KEY_AXES = ("y", "c")
ROW_AXES = ("x",)
ALL_AXES = ("x", "zl", "y", "zh", "c")


def exchange(array, axes):
    return lax.all_to_all(array, axes, split_axis=0, concat_axis=0, tiled=True)


def shards(queries, keys, values):
    groups = lax.axis_size(HEAD_AXES)
    blocks = lax.axis_size(ROW_AXES)
    rows, columns = queries.shape
    width = columns // groups
    kv = exchange(split(groups, keys, values), HEAD_AXES)
    kv = lax.all_gather(kv, KEY_AXES, axis=0, tiled=True)
    q = exchange(split(groups, queries), HEAD_AXES).reshape(1, groups * rows, width)
    q = exchange(jnp.broadcast_to(q, (blocks, groups * rows, width)), ROW_AXES)
    parts = attend(q, kv)
    merged = merge(exchange(parts, ROW_AXES)).reshape(groups, rows, width)
    spread = exchange(merged, HEAD_AXES)
    return spread.transpose(1, 0, 2).reshape(rows, columns)


def solution(mesh):
    fine = Mesh(mesh.devices.reshape(4, 2, 8, 4, 2), ALL_AXES)
    placed = P(ALL_AXES, None)
    return jax.shard_map(
        shards, mesh=fine, in_specs=(placed,) * 3, out_specs=placed, check_vma=False
    )
```

```python
import functools
import math

import jax
import jax.numpy as jnp
from jax import lax
from jax.experimental import pallas as pl
from jax.experimental.pallas import tpu as pltpu
from jax.sharding import Mesh, PartitionSpec as P

HEAD_DIM = 128
STAT_ROWS = 16
KEY_CHUNK = 512
EXPONENT = HEAD_DIM**-0.5 * math.log2(math.e)


def head_cols(h):
    return slice(h * HEAD_DIM, (h + 1) * HEAD_DIM)


def attend_kernel(q_ref, kv_ref, out_ref, held_ref, copied, score_a, score_b):
    score_refs = (score_a, score_b)
    blocks, rows, width = q_ref.shape
    heads = width // HEAD_DIM
    unit_rows = score_a.shape[0]
    per_unit = unit_rows // rows
    units = blocks // per_unit
    run = held_ref.shape[2]
    step = KEY_CHUNK // run
    chunks = held_ref.shape[0] // (2 * step)

    def copy(j):
        part = pl.ds(j * step, step)
        return pltpu.make_async_copy(kv_ref.at[part], held_ref.at[part], copied.at[j])

    def kv_chunk(which, h, j):
        block = held_ref[j * step : (j + 1) * step, which, :, head_cols(h)]
        return block.reshape(KEY_CHUNK, HEAD_DIM)

    def query(i, h):
        block = q_ref[pl.ds(i * per_unit, per_unit), :, head_cols(h)]
        return block.reshape(unit_rows, HEAD_DIM)

    def cols_of(j):
        return slice(j * KEY_CHUNK, (j + 1) * KEY_CHUNK)

    def score_chunk(q, h, half, slot, j, top):
        k = kv_chunk(0, h, half * chunks + j)
        s = lax.dot_general(q, k, (((1,), (1,)), ((), ())), preferred_element_type=jnp.float32)
        score_refs[slot][:, cols_of(j)] = s
        for t in range(KEY_CHUNK // HEAD_DIM):
            part = s[:, head_cols(t)]
            top = part if top is None else jnp.maximum(top, part)
        return top

    def shift_of(top):
        best = jnp.max(top, axis=1, keepdims=True) * EXPONENT
        return best.astype(jnp.bfloat16).astype(jnp.float32)

    for j in range(2 * chunks):
        copy(j).start()
    ones = jnp.ones((KEY_CHUNK, HEAD_DIM), jnp.bfloat16)
    order = [(half, h) for half in range(2) for h in range(heads)]
    top = None
    q = query(0, 0)
    for j in range(chunks):
        copy(j).wait()
        top = score_chunk(q, 0, 0, 0, j, top)

    def rows_step(i, shift):
        lane = lax.broadcasted_iota(jnp.int32, (unit_rows, HEAD_DIM), 1)
        stats = jnp.zeros((unit_rows, HEAD_DIM), jnp.float32)
        held = {}
        for n, (half, h) in enumerate(order):
            if n == heads - 1:

                @pl.when(i == 0)
                def _():
                    for j in range(chunks, 2 * chunks):
                        copy(j).wait()

            wraps = n + 1 == len(order)
            next_half, next_h = order[(n + 1) % len(order)]
            q = query(jnp.minimum(i + 1, units - 1) if wraps else i, next_h)
            if half:
                shift_before, total_before = held[h]
                shift = jnp.maximum(shift, shift_before)
            top, total, waiting = None, None, None
            for j in range(chunks + 1):
                if j < chunks:
                    top = score_chunk(q, next_h, next_half, (n + 1) % 2, j, top)
                if j == chunks - 1:
                    shift_after = shift_of(top)
                if j > 0:
                    v = jnp.concatenate([kv_chunk(1, h, half * chunks + j - 1), ones], axis=1)
                    o = jnp.dot(waiting, v, preferred_element_type=jnp.float32)
                    total = o if total is None else total + o
                if j < chunks:
                    s = score_refs[n % 2][:, cols_of(j)]
                    waiting = jnp.exp2(s * EXPONENT - shift).astype(jnp.bfloat16)
            if half:
                total = total + jnp.exp2(shift_before - shift) * total_before
                for b in range(per_unit):
                    part = total[b * rows : (b + 1) * rows, 0:HEAD_DIM].astype(jnp.bfloat16)
                    out_ref[i * per_unit + b, 0:rows, head_cols(h)] = part
                denom = total[:, HEAD_DIM:]
                high = denom.astype(jnp.bfloat16).astype(jnp.float32)
                stats = jnp.where(lane == h, shift, stats)
                stats = jnp.where(lane == heads + h, high, stats)
                stats = jnp.where(lane == 2 * heads + h, denom - high, stats)
            else:
                held[h] = shift, total
            shift = shift_after
        flipped = stats.T[0:STAT_ROWS].astype(jnp.bfloat16)
        blank = jnp.zeros((STAT_ROWS, width - rows), jnp.bfloat16)
        for b in range(per_unit):
            block = i * per_unit + b
            out_ref[block, rows:, 0:rows] = flipped[:, b * rows : (b + 1) * rows]
            out_ref[block, rows:, rows:] = blank
        return shift

    lax.fori_loop(0, units, rows_step, shift_of(top))


def attend(q, kv):
    blocks, rows, width = q.shape
    heads = width // HEAD_DIM
    keys_n = kv.shape[0] * kv.shape[2]
    vmem = pl.BlockSpec(memory_space=pltpu.VMEM)
    unit_rows = 2 * rows
    return pl.pallas_call(
        attend_kernel,
        in_specs=[vmem, pl.BlockSpec(memory_space=pl.ANY)],
        out_specs=vmem,
        out_shape=jax.ShapeDtypeStruct((blocks, rows + STAT_ROWS, width), jnp.bfloat16),
        scratch_shapes=[
            pltpu.VMEM(kv.shape, kv.dtype),
            pltpu.SemaphoreType.DMA((keys_n // KEY_CHUNK,)),
            pltpu.VMEM((unit_rows, keys_n // 2), jnp.float32),
            pltpu.VMEM((unit_rows, keys_n // 2), jnp.float32),
        ],
        compiler_params=pltpu.CompilerParams(vmem_limit_bytes=56 * 2**20),
        cost_estimate=pl.CostEstimate(
            flops=4 * blocks * rows * keys_n * width,
            bytes_accessed=4 * (blocks * rows * width + keys_n * width),
            transcendentals=blocks * rows * keys_n * heads,
        ),
    )(q, kv)


def merge_kernel(parts_ref, out_ref):
    pieces = parts_ref.shape[0]
    rows, width = out_ref.shape
    heads = width // HEAD_DIM
    stats = [
        parts_ref[p, rows : rows + STAT_ROWS, 0:rows].astype(jnp.float32) for p in range(pieces)
    ]
    shifts = [s[0:heads] for s in stats]
    totals = [s[heads : 2 * heads] + s[2 * heads : 3 * heads] for s in stats]
    best = functools.reduce(jnp.maximum, shifts)
    factors = [jnp.exp2(s - best) for s in shifts]
    denom = sum(f * t for f, t in zip(factors, totals))
    weights = jnp.concatenate([f / denom for f in factors], axis=0)
    pad = jnp.zeros((HEAD_DIM - weights.shape[0], rows), jnp.float32)
    weights = jnp.concatenate([weights, pad], axis=0).T
    for h in range(heads):
        total = jnp.zeros((rows, HEAD_DIM), jnp.float32)
        for p in range(pieces):
            w = weights[:, p * heads + h : p * heads + h + 1]
            total = total + w * parts_ref[p, 0:rows, head_cols(h)].astype(jnp.float32)
        out_ref[:, head_cols(h)] = total.astype(jnp.bfloat16)


def merge(parts):
    pieces, part_rows, width = parts.shape
    return pl.pallas_call(
        merge_kernel,
        out_shape=jax.ShapeDtypeStruct((part_rows - STAT_ROWS, width), jnp.bfloat16),
        in_specs=[pl.BlockSpec(memory_space=pltpu.VMEM)],
        out_specs=pl.BlockSpec(memory_space=pltpu.VMEM),
        compiler_params=pltpu.CompilerParams(vmem_limit_bytes=32 * 2**20),
    )(parts)


def split_kernel(*refs):
    *in_refs, out_ref = refs
    groups, arrays, rows, width = out_ref.shape
    for g in range(groups):
        for a in range(arrays):
            out_ref[g, a] = in_refs[a][:, g * width : (g + 1) * width]


def split(groups, *arrays):
    rows, columns = arrays[0].shape
    return pl.pallas_call(
        split_kernel,
        out_shape=jax.ShapeDtypeStruct(
            (groups, len(arrays), rows, columns // groups), arrays[0].dtype
        ),
        in_specs=[pl.BlockSpec(memory_space=pltpu.VMEM)] * len(arrays),
        out_specs=pl.BlockSpec(memory_space=pltpu.VMEM),
    )(*arrays)


HEAD_AXES = ("zh", "zl")
KEY_AXES = ("y", "c")
ROW_AXES = ("x",)
ALL_AXES = ("x", "zl", "y", "zh", "c")


def exchange(array, axes):
    return lax.all_to_all(array, axes, split_axis=0, concat_axis=0, tiled=True)


def shards(queries, keys, values):
    groups = lax.axis_size(HEAD_AXES)
    blocks = lax.axis_size(ROW_AXES)
    rows, columns = queries.shape
    width = columns // groups
    kv = exchange(split(groups, keys, values), HEAD_AXES)
    kv = lax.all_gather(kv, KEY_AXES, axis=0, tiled=True)
    q = exchange(split(groups, queries), HEAD_AXES).reshape(1, groups * rows, width)
    q = exchange(jnp.broadcast_to(q, (blocks, groups * rows, width)), ROW_AXES)
    parts = attend(q, kv)
    merged = merge(exchange(parts, ROW_AXES)).reshape(groups, rows, width)
    spread = exchange(merged, HEAD_AXES)
    return spread.transpose(1, 0, 2).reshape(rows, columns)


def solution(mesh):
    fine = Mesh(mesh.devices.reshape(4, 2, 8, 4, 2), ALL_AXES)
    placed = P(ALL_AXES, None)
    return jax.shard_map(
        shards, mesh=fine, in_specs=(placed,) * 3, out_specs=placed, check_vma=False
    )
```
